512 devices in a mesh: layer: 4 (over y), row: 16 (over z_lo, core), col: 8 (over z_hi, x).
Axes of the slice: x: 4, y: 4, z: 16 (z_hi: 2, z_lo: 8; z = z_hi * 8 + z_lo), core: 2. Of those that a mesh axis runs over, the one named last changes fastest.
Arguments:
- intermediate: float32 [8192, 65536], P('col', ('layer', 'row')), may hold values from -0.0625 to 0.0625
- amplitudes: float32 [65536, 1024], P(('layer', 'row', 'col')), may hold values from -24 to 24
- occ_irrep: int32 [200], replicated, may hold values from 0 to 7
- vir_irrep: int32 [1800], replicated, may hold values from 0 to 7, as said below
Outputs:
- cycle_term: float32 [1024, 8192], P(('layer', 'row'), 'col')
The draws below stay inside these ranges and needn't reach their ends.
Inputs may be any that keep to these rules, and one draw needn't show every extreme that they name: `vir_irrep`: in each aligned run of 8 virtual orbitals (0 to 7, 8 to 15, and so on) every irrep 0 to 7 occurs exactly once.
All inputs are finite; a program needn't handle non-finite values.
Results may differ from the reference program's by a relative error of at most 0.0003.
Values sent between devices are 32-bit elements; how exact they have to be, the bound alone decides.
A program may use at most 64 MiB of HBM per device.

```python
import jax
import jax.numpy as jnp
from jax import lax

OCC = 200
VIRT = 1800
M_DEV = 1024
COLS = 1024
ROWS = 8192
CYCLE = 65536


def draw_vir_irrep(key, part):
    key = jax.random.fold_in(key, 5)
    keys = jax.random.split(key, VIRT // 8)
    orders = jax.vmap(lambda single: jax.random.permutation(single, 8))(keys)
    return orders.reshape(VIRT).astype(jnp.int32)


def touch_ends(array, stream_key, low, largest):
    dims = array.shape
    place = [jax.random.randint(jax.random.fold_in(stream_key, axis), (), 0, dims[axis]) for axis in range(len(dims))]
    array = array.at[tuple(place)].set(low)
    longest = dims.index(max(dims))
    place[longest] = (place[longest] + 1) % dims[longest]
    return array.at[tuple(place)].set(largest)


def raised(array, rng, source, target, parts, factor):
    def block_of(dim):
        return (jnp.arange(array.shape[dim]) // (array.shape[dim] // parts)).reshape((-1,) + (1,) * (array.ndim - 1 - dim))

    near = jax.random.permutation(rng, parts)[block_of(target)]
    other_side = (block_of(target) + parts // 2) % parts
    return jnp.where((block_of(source) == near) | (block_of(source) == other_side), factor * array, array)


def steps_of(stream_key, extent, shards, low, high):
    gain, own = 1.0, jax.random.fold_in(stream_key, 6)
    for axis_at, blocks in shards:
        heights = jnp.exp(jax.random.uniform(jax.random.fold_in(own, axis_at), (blocks,), jnp.float32, low / len(shards), high / len(shards)))
        gain = gain * jnp.repeat(heights, extent[axis_at] // blocks).reshape([-1 if axis == axis_at else 1 for axis in range(len(extent))])
    return gain


def gaussian(stream_key, shape, width, most, cuts=(), held_as=jnp.bfloat16):
    factor_of = steps_of(stream_key, shape, cuts, -0.22, 0.18) if cuts else 1.0
    array = jax.random.normal(stream_key, shape, jnp.float32) * width * factor_of
    return jnp.minimum(jnp.maximum(array, -most), most).astype(held_as)


def heavy_noise(rng, extent, scale, limit, cuts, heavy, kind=jnp.bfloat16):
    values = scale * jax.random.normal(rng, extent, jnp.float32)
    if cuts:
        values = values * steps_of(rng, extent, cuts, -0.22, 0.18)
    return jnp.clip(raised(values, jax.random.fold_in(rng, 3), *heavy), -limit, limit).astype(kind)


def setup_inputs(seed: int = 0) -> dict:
    splits = jax.random.split(jax.random.key(seed), 5)
    intermediate = gaussian(splits[0], (ROWS, CYCLE), (CYCLE // 8) ** -0.5, 0.0625, ((0, 8), (1, 64)), jnp.float32)
    amplitudes = heavy_noise(splits[1], (CYCLE, COLS), 1.0, 24.0, ((0, 512),), (0, 1, 512, 6.0), jnp.float32)
    occ_irrep = touch_ends(jax.random.randint(splits[2], (OCC,), 0, 8), jax.random.fold_in(splits[2], 1), 0, 7).astype(jnp.int32)
    vir_irrep = draw_vir_irrep(jax.random.fold_in(splits[4], 71), 0)
    return {"intermediate": intermediate, "amplitudes": amplitudes, "occ_irrep": occ_irrep, "vir_irrep": vir_irrep}


def pair_irreps(offset, count, occ_irrep, vir_irrep):
    indices = offset + jnp.arange(count, dtype=jnp.int32)
    groups = indices // 8
    occupied = jnp.take(occ_irrep, groups % OCC)
    virtual = jnp.take(vir_irrep, 8 * (groups // OCC) + indices % 8)
    return jnp.bitwise_xor(occupied, virtual)


def reference(intermediate, amplitudes, occ_irrep, vir_irrep):
    cycle_irreps = pair_irreps(0, CYCLE, occ_irrep, vir_irrep)
    col_irreps = pair_irreps(0, COLS, occ_irrep, vir_irrep)
    nblocks = ROWS // M_DEV
    blocks = intermediate.reshape(nblocks, M_DEV, CYCLE)
    numbers = jnp.arange(nblocks, dtype=jnp.int32)

    def one_block(packed):
        block, number = packed
        row_irreps = pair_irreps(number * M_DEV, M_DEV, occ_irrep, vir_irrep)
        masked = jnp.where(row_irreps[:, None] == cycle_irreps[None, :], block, jnp.zeros_like(block))
        product = lax.dot_general(amplitudes, masked, (((0,), (1,)), ((), ())),
                                  precision=lax.Precision.HIGHEST, preferred_element_type=jnp.float32)
        return jnp.where(col_irreps[:, None] == row_irreps[None, :], product, jnp.zeros_like(product))

    results = lax.map(one_block, (blocks, numbers))
    return jnp.transpose(results, (1, 0, 2)).reshape(COLS, ROWS)
```

```python
import jax
import jax.numpy as jnp
from jax import lax
from jax.experimental import pallas as pl
from jax.experimental.pallas import tpu as pltpu
from jax.sharding import PartitionSpec as P

MESH = pl.DeviceIdType.MESH
OCC = 200
IRREPS = 8
LANES = 128
W_CHUNKS = 8


def take_lanes(values, index):
    return jnp.take_along_axis(values, index, axis=1)


def take_rows(values, index):
    return jnp.take_along_axis(values, index, axis=0)


def run_tables(first, offset, occ_low, occ_high, vir_ref, sub):
    virtual = first // OCC
    orbital = first % OCC + offset
    wraps = orbital >= OCC
    orbital = jnp.where(wraps, orbital - OCC, orbital)
    low = take_lanes(occ_low, orbital & (LANES - 1))
    high = take_lanes(occ_high, orbital & (LANES - 1))
    occupied = jnp.where(orbital < LANES, low, high)
    irrep = jnp.zeros_like(sub)
    place = jnp.zeros_like(sub)
    for s in range(IRREPS):
        here = vir_ref[IRREPS * virtual + s]
        after = vir_ref[IRREPS * (virtual + 1) + s]
        value = occupied ^ jnp.where(wraps, after, here)
        irrep = jnp.where(sub == s, value, irrep)
        place = jnp.where(value == sub, s, place)
    return irrep, place


def split(values):
    high = values.astype(jnp.bfloat16)
    low = (values - high.astype(jnp.float32)).astype(jnp.bfloat16)
    return high, low


def kernel(
    w_hbm, a_hbm, occ_ref, vir_ref, out_ref,
    w_raw, a_raw, a_all, w_c, part, core_in, y_out, y_in, z_out, z_in,
    load_sem, col_send, col_recv, red_send, red_recv,
):
    layer, row, col = lax.axis_index("layer"), lax.axis_index("row"), lax.axis_index("col")
    core, z_lo = row % 2, row // 2
    z_hi, x = col // 4, col % 4

    def at(layer_=layer, z_lo_=z_lo, core_=core, col_=col):
        return (layer_, z_lo_ * 2 + core_, col_)

    far_col = (1 - z_hi) * 4 + x
    far = at(col_=far_col)
    x_cols = [z_hi * 4 + (x + k) % 4 for k in range(1, 4)]
    x_peers = [at(col_=c) for c in x_cols]
    y_peers = [at(layer_=(layer + k) % 4) for k in range(1, 4)]
    z_peers = [at(z_lo_=(z_lo + k) % 8) for k in range(1, 8)]
    core_peer = at(core_=1 - core)
    peers = [far, core_peer] + x_peers + y_peers + z_peers

    barrier = pltpu.get_barrier_semaphore()
    for peer in peers:
        pl.semaphore_signal(barrier, inc=1, device_id=peer, device_id_type=MESH)

    a_load = pltpu.make_async_copy(a_hbm, a_raw, load_sem.at[W_CHUNKS])
    a_load.start()
    chunk_rows = w_raw.shape[0] // W_CHUNKS
    w_loads = [
        pltpu.make_async_copy(
            w_hbm.at[pl.ds(n * chunk_rows, chunk_rows)], w_raw.at[pl.ds(n * chunk_rows, chunk_rows)], load_sem.at[n]
        )
        for n in range(W_CHUNKS)
    ]
    for load in w_loads:
        load.start()

    shape = (IRREPS, LANES)
    sub = lax.broadcasted_iota(jnp.int32, shape, 0)
    lane = lax.broadcasted_iota(jnp.int32, shape, 1)
    occ_low = jnp.broadcast_to(occ_ref[0:1, :], shape)
    occ_high = jnp.broadcast_to(occ_ref[1:2, :], shape)
    run_of = ((lane >> 4) & 3) * 32 + ((lane >> 1) & 7) * 4 + (lane >> 6) * 2 + (lane & 1)
    n_irrep, n_place = run_tables(0, run_of, occ_low, occ_high, vir_ref, sub)
    p_irrep, p_place = run_tables((layer * 16 + row) * LANES, lane, occ_low, occ_high, vir_ref, sub)
    m_irrep, m_place = run_tables(col * LANES, lane, occ_low, occ_high, vir_ref, sub)

    def compact(raw_ref, first_row, irrep, place, run, lane_index, block):
        which = jnp.full(shape, run, jnp.int32)
        index = take_rows(lane_index, take_lanes(irrep, which))
        total = jnp.zeros(shape, jnp.float32)
        for k in range(IRREPS):
            values = raw_ref[pl.ds(first_row, IRREPS), pl.ds(k * LANES, LANES)]
            total = jnp.where(block == k, take_lanes(values, index), total)
        return take_rows(total, take_lanes(place, which))

    a_load.wait()
    n_index, n_block = 8 * (run_of & 15) + n_place, run_of >> 4

    def compact_a(j, _):
        rows = pl.multiple_of(j * IRREPS, IRREPS)
        a_all[pl.ds(pl.multiple_of(col * LANES + rows, IRREPS), IRREPS), :] = compact(
            a_raw, rows, p_irrep, p_place, 16 * col + j, n_index, n_block
        )
        return 0

    lax.fori_loop(0, 16, compact_a, 0, unroll=4)

    p_index, p_block = 8 * (lane & 15) + p_place, lane >> 4

    def compact_w(i, _):
        rows = pl.multiple_of(i * IRREPS, IRREPS)
        w_c[pl.ds(rows, IRREPS), :] = compact(w_raw, rows, m_irrep, m_place, i, p_index, p_block)
        return 0

    for n in range(W_CHUNKS):
        w_loads[n].wait()
        runs = LANES // W_CHUNKS
        lax.fori_loop(n * runs, (n + 1) * runs, compact_w, 0, unroll=4)

    pl.semaphore_wait(barrier, len(peers))

    def block(c):
        return a_all.at[pl.ds(pl.multiple_of(c * LANES, LANES), LANES)]

    def col_copy(c, n, peer):
        return pltpu.make_async_remote_copy(
            src_ref=block(c), dst_ref=block(c), send_sem=col_send.at[n], recv_sem=col_recv.at[n],
            device_id=peer, device_id_type=MESH,
        )

    sends = [col_copy(col, 0, far)] + [col_copy(col, 1 + k, x_peers[k]) for k in range(3)]
    for copy in sends:
        copy.start()
    col_copy(far_col, 0, far).wait_recv()
    passes = [col_copy(far_col, 4 + k, x_peers[k]) for k in range(3)]
    for copy in passes:
        copy.start()
    for k in range(3):
        source = (x + 3 - k) % 4
        col_copy(z_hi * 4 + source, 1 + k, x_peers[k]).wait_recv()
        col_copy((1 - z_hi) * 4 + source, 4 + k, x_peers[k]).wait_recv()

    for g in range(IRREPS):
        a_high, a_low = split(a_all[pl.ds(g, LANES, stride=IRREPS), :].T)
        w_high, w_low = split(w_c[pl.ds(g, LANES, stride=IRREPS), :])

        def product(left, right):
            return lax.dot_general(left, right, (((1,), (1,)), ((), ())), preferred_element_type=jnp.float32)

        total = product(a_low, w_high) + product(a_high, w_low) + product(a_high, w_high)
        part[0, g] = total[:64]
        part[1, g] = total[64:]

    def red_copy(source, target, n, peer):
        return pltpu.make_async_remote_copy(
            src_ref=source, dst_ref=target, send_sem=red_send.at[n], recv_sem=red_recv.at[n],
            device_id=peer, device_id_type=MESH,
        )

    copy = red_copy(part.at[1 - core], core_in, 0, core_peer)
    copy.start()
    sends.append(copy)
    copy.wait_recv()
    for g in range(IRREPS):
        total = part[core, g] + core_in[g]
        for k in range(4):
            y_out[k, g] = total[16 * k : 16 * k + 16]

    y_copies = [red_copy(y_out.at[(layer + k) % 4], y_in.at[k - 1], k, y_peers[k - 1]) for k in range(1, 4)]
    for copy in y_copies:
        copy.start()
    for copy in y_copies:
        copy.wait_recv()
    for g in range(IRREPS):
        total = y_out[layer, g] + y_in[0, g] + y_in[1, g] + y_in[2, g]
        z_out[pl.ds(g, 16, stride=IRREPS), :] = total

    def z_rows(z):
        return pl.ds(pl.multiple_of(z * 16, 16), 16)

    z_copies = [red_copy(z_out.at[z_rows((z_lo + k) % 8)], z_in.at[k - 1], 3 + k, z_peers[k - 1]) for k in range(1, 8)]
    for copy in z_copies:
        copy.start()
    for copy in z_copies:
        copy.wait_recv()
    total = z_out[z_rows(z_lo), :]
    for k in range(7):
        total = total + z_in[k]

    first_lane = core * 64 + layer * 16 + z_lo * 2
    for e in range(2):
        order = take_lanes(n_irrep, jnp.full(shape, first_lane + e, jnp.int32))
        for k in range(IRREPS):
            spread = 16 * k + (lane >> 3)
            kept = take_lanes(m_place, spread) == (lane & 7)
            values = jnp.where(kept, take_lanes(total[8 * e : 8 * e + 8], spread), 0.0)
            out_ref[8 * e : 8 * e + 8, k * LANES : (k + 1) * LANES] = take_rows(values, order)

    for copy in sends + passes + y_copies + z_copies:
        copy.wait_send()


def per_device(intermediate, amplitudes, occ_irrep, vir_irrep):
    occupied = jnp.pad(occ_irrep, (0, 2 * LANES - OCC)).reshape(2, LANES)
    vmem = pltpu.VMEM
    f32 = jnp.float32
    return pl.pallas_call(
        kernel,
        out_shape=jax.ShapeDtypeStruct((16, 1024), f32),
        in_specs=[
            pl.BlockSpec(memory_space=pl.ANY),
            pl.BlockSpec(memory_space=pl.ANY),
            pl.BlockSpec(memory_space=vmem),
            pl.BlockSpec(memory_space=pltpu.SMEM),
        ],
        out_specs=pl.BlockSpec(memory_space=vmem),
        scratch_shapes=[
            vmem((1024, 1024), f32),
            vmem((128, 1024), f32),
            vmem((1024, LANES), f32),
            vmem((1024, LANES), f32),
            vmem((2, IRREPS, 64, LANES), f32),
            vmem((IRREPS, 64, LANES), f32),
            vmem((4, IRREPS, 16, LANES), f32),
            vmem((3, IRREPS, 16, LANES), f32),
            vmem((LANES, LANES), f32),
            vmem((7, 16, LANES), f32),
            pltpu.SemaphoreType.DMA((W_CHUNKS + 1,)),
            pltpu.SemaphoreType.DMA((7,)),
            pltpu.SemaphoreType.DMA((7,)),
            pltpu.SemaphoreType.DMA((11,)),
            pltpu.SemaphoreType.DMA((11,)),
        ],
        compiler_params=pltpu.CompilerParams(
            collective_id=0, has_side_effects=True, vmem_limit_bytes=60 * 1024 * 1024
        ),
        name="cycle_contraction",
    )(intermediate, amplitudes, occupied, vir_irrep)


def solution(mesh):
    return jax.shard_map(
        per_device,
        mesh=mesh,
        in_specs=(P("col", ("layer", "row")), P(("layer", "row", "col"), None), P(), P()),
        out_specs=P(("layer", "row"), "col"),
        check_vma=False,
    )
```

```python
import jax
import jax.numpy as jnp
from jax import lax
from jax.experimental import pallas as pl
from jax.experimental.pallas import tpu as pltpu
from jax.sharding import PartitionSpec as P

MESH = pl.DeviceIdType.MESH
OCC = 200
IRREPS = 8
LANES = 128
W_CHUNKS = 8
FAR_CHUNKS = 2


def take_lanes(values, index):
    return jnp.take_along_axis(values, index, axis=1)


def take_rows(values, index):
    return jnp.take_along_axis(values, index, axis=0)


def run_tables(first, offset, occ_low, occ_high, vir_ref, sub):
    virtual = first // OCC
    orbital = first % OCC + offset
    wraps = orbital >= OCC
    orbital = jnp.where(wraps, orbital - OCC, orbital)
    low = take_lanes(occ_low, jnp.minimum(orbital, LANES - 1))
    high = take_lanes(occ_high, jnp.maximum(orbital - (OCC - LANES), 0))
    occupied = jnp.where(orbital < LANES, low, high)
    irrep = jnp.zeros_like(sub)
    place = jnp.zeros_like(sub)
    for s in range(IRREPS):
        here = vir_ref[IRREPS * virtual + s]
        after = vir_ref[IRREPS * (virtual + 1) + s]
        value = occupied ^ jnp.where(wraps, after, here)
        irrep = jnp.where(sub == s, value, irrep)
        place = jnp.where(value == sub, s, place)
    return irrep, place


def split(values):
    high = values.astype(jnp.bfloat16)
    low = (values - high.astype(jnp.float32)).astype(jnp.bfloat16)
    return high, low


def kernel(
    w_hbm, a_hbm, occ_ref, vir_ref, out_ref,
    w_raw, a_raw, a_all, w_c, part, core_in, y_out, y_in, z_out, z_in,
    load_sem, col_send, col_recv, red_send, red_recv, known,
):
    layer, row, col = lax.axis_index("layer"), lax.axis_index("row"), lax.axis_index("col")
    core, z_lo = row % 2, row // 2
    z_hi, x = col // 4, col % 4

    def at(layer_=layer, z_lo_=z_lo, core_=core, col_=col):
        return (layer_, z_lo_ * 2 + core_, col_)

    def signal(semaphore, peer):
        pl.semaphore_signal(semaphore, inc=1, device_id=peer, device_id_type=MESH)

    far_col = (1 - z_hi) * 4 + x
    far, middle = at(col_=far_col), at(z_lo_=z_lo + 4 - 8 * (z_lo // 4))
    x_peers = [at(col_=z_hi * 4 + (x + k) % 4) for k in range(1, 4)]
    y_peers = [at(layer_=(layer + k) % 4) for k in range(1, 4)]
    z_peers = [at(z_lo_=(z_lo + k) % 8) for k in range(1, 8)]
    core_peer = at(core_=1 - core)
    z_near = [at(z_lo_=z_lo + 1 - 2 * (z_lo % 2)), at(z_lo_=z_lo + 2 - 4 * (z_lo // 2 % 2)), middle]
    near = z_near + [core_peer, far] + x_peers + y_peers

    barrier = pltpu.get_barrier_semaphore()
    for peer in near:
        signal(barrier, peer)

    a_load = pltpu.make_async_copy(a_hbm, a_raw, load_sem.at[W_CHUNKS])
    a_load.start()
    chunk_rows = w_raw.shape[0] // W_CHUNKS

    def w_load(n):
        rows = pl.ds(pl.multiple_of(n * chunk_rows, chunk_rows), chunk_rows)
        return pltpu.make_async_copy(w_hbm.at[rows], w_raw.at[rows], load_sem.at[n])

    shape = (IRREPS, LANES)
    sub = lax.broadcasted_iota(jnp.int32, shape, 0)
    lane = lax.broadcasted_iota(jnp.int32, shape, 1)
    occ_low = jnp.broadcast_to(occ_ref[pl.ds(0, LANES)][None, :], shape)
    occ_high = jnp.broadcast_to(occ_ref[pl.ds(OCC - LANES, LANES)][None, :], shape)
    run_of = ((lane >> 4) & 3) * 32 + ((lane >> 1) & 7) * 4 + (lane >> 6) * 2 + (lane & 1)
    n_irrep, n_place = run_tables(0, run_of, occ_low, occ_high, vir_ref, sub)
    p_irrep, p_place = run_tables((layer * 16 + row) * LANES, lane, occ_low, occ_high, vir_ref, sub)
    m_irrep, m_place = run_tables(col * LANES, lane, occ_low, occ_high, vir_ref, sub)

    def compact(raw_ref, first_row, irrep, place, run, lane_index, block):
        which = jnp.full(shape, run, jnp.int32)
        index = take_rows(lane_index, take_lanes(irrep, which))
        total = jnp.zeros(shape, jnp.float32)
        for k in range(IRREPS):
            values = raw_ref[pl.ds(first_row, IRREPS), pl.ds(k * LANES, LANES)]
            total = jnp.where(block == k, take_lanes(values, index), total)
        return take_rows(total, take_lanes(place, which))

    a_load.wait()
    for n in range(W_CHUNKS):
        w_load(n).start()
    n_index, n_block = 8 * (run_of & 15) + n_place, run_of >> 4

    def compact_a(j, _):
        rows = pl.multiple_of(j * IRREPS, IRREPS)
        a_all[pl.ds(pl.multiple_of(col * LANES + rows, IRREPS), IRREPS), :] = compact(
            a_raw, rows, p_irrep, p_place, 16 * col + j, n_index, n_block
        )
        return 0

    lax.fori_loop(0, 16, compact_a, 0, unroll=8)

    pl.semaphore_wait(barrier, len(near))

    far_rows = LANES // FAR_CHUNKS
    x_at, far_at, pass_at = 0, 3, 3 + FAR_CHUNKS

    def block(ref, c, n=None):
        start, rows = (0, LANES) if n is None else (n * far_rows, far_rows)
        return ref.at[pl.ds(pl.multiple_of(c * LANES + start, far_rows), rows)]

    def col_copy(source, target, n, peer):
        return pltpu.make_async_remote_copy(
            src_ref=source, dst_ref=target, send_sem=col_send.at[n], recv_sem=col_recv.at[n],
            device_id=peer, device_id_type=MESH,
        )

    to_far = [col_copy(block(a_all, col, n), block(a_all, col, n), far_at + n, far) for n in range(FAR_CHUNKS)]
    own_x = [col_copy(block(a_all, col), block(a_all, col), x_at + k, x_peers[k]) for k in range(3)]

    for copy in to_far:
        copy.start()
    for copy in own_x:
        copy.start()
    for peer in z_near:
        signal(known.at[0], peer)

    p_index, p_block = 8 * (lane & 15) + p_place, lane >> 4

    def compact_w(i, _):
        rows = pl.multiple_of(i * IRREPS, IRREPS)
        w_c[pl.ds(rows, IRREPS), :] = compact(w_raw, rows, m_irrep, m_place, i, p_index, p_block)
        return 0

    def compact_chunk(n, _):
        w_load(n).wait()
        runs = LANES // W_CHUNKS
        for i in range(runs):
            compact_w(n * runs + i, 0)
        return 0

    lax.fori_loop(0, W_CHUNKS, compact_chunk, 0)

    pl.semaphore_wait(known.at[0], len(z_near))
    for peer in z_near:
        signal(known.at[1], peer)

    passes = []
    for n in range(FAR_CHUNKS):
        col_copy(block(a_all, far_col, n), block(a_all, far_col, n), far_at + n, far).wait_recv()
        for k in range(3):
            copy = col_copy(
                block(a_all, far_col, n), block(a_all, far_col, n), pass_at + 3 * n + k, x_peers[k]
            )
            copy.start()
            passes.append(copy)
    for k in range(3):
        source = (x + 3 - k) % 4
        mine = block(a_all, z_hi * 4 + source)
        col_copy(mine, mine, x_at + k, x_peers[k]).wait_recv()
        for n in range(FAR_CHUNKS):
            passed = block(a_all, (1 - z_hi) * 4 + source, n)
            col_copy(passed, passed, pass_at + 3 * n + k, x_peers[k]).wait_recv()

    def multiply(g, _):
        a_high, a_low = split(a_all[pl.ds(g, LANES, stride=IRREPS), :].T)
        w_high, w_low = split(w_c[pl.ds(g, LANES, stride=IRREPS), :])

        def product(left, right):
            return lax.dot_general(left, right, (((1,), (1,)), ((), ())), preferred_element_type=jnp.float32)

        total = product(a_low, w_high) + product(a_high, w_low) + product(a_high, w_high)
        part[0, g] = total[:64]
        part[1, g] = total[64:]
        return 0

    lax.fori_loop(0, IRREPS, multiply, 0, unroll=2)

    def red_copy(source, target, n, peer):
        return pltpu.make_async_remote_copy(
            src_ref=source, dst_ref=target, send_sem=red_send.at[n], recv_sem=red_recv.at[n],
            device_id=peer, device_id_type=MESH,
        )

    core_copy = red_copy(part.at[1 - core], core_in, 0, core_peer)
    core_copy.start()
    core_copy.wait_recv()
    def add_core(g, _):
        total = part[core, g] + core_in[g]
        for k in range(4):
            y_out[k, g] = total[16 * k : 16 * k + 16]
        return 0

    lax.fori_loop(0, IRREPS, add_core, 0)

    y_copies = [red_copy(y_out.at[(layer + k) % 4], y_in.at[k - 1], k, y_peers[k - 1]) for k in range(1, 4)]
    for copy in y_copies:
        copy.start()
    for copy in y_copies:
        copy.wait_recv()
    for g in range(IRREPS):
        total = y_out[layer, g] + y_in[0, g] + y_in[1, g] + y_in[2, g]
        z_out[pl.ds(g, 16, stride=IRREPS), :] = total

    pl.semaphore_wait(known.at[1], len(z_near))

    def z_rows(z):
        return pl.ds(pl.multiple_of(z * 16, 16), 16)

    z_copies = [red_copy(z_out.at[z_rows((z_lo + k) % 8)], z_in.at[k - 1], 3 + k, z_peers[k - 1]) for k in range(1, 8)]
    for copy in z_copies:
        copy.start()
    for copy in z_copies:
        copy.wait_recv()
    total = z_out[z_rows(z_lo), :]
    for k in range(7):
        total = total + z_in[k]

    first_lane = core * 64 + layer * 16 + z_lo * 2
    for e in range(2):
        order = take_lanes(n_irrep, jnp.full(shape, first_lane + e, jnp.int32))
        for k in range(IRREPS):
            spread = 16 * k + (lane >> 3)
            kept = take_lanes(m_place, spread) == (lane & 7)
            values = jnp.where(kept, take_lanes(total[8 * e : 8 * e + 8], spread), 0.0)
            out_ref[8 * e : 8 * e + 8, k * LANES : (k + 1) * LANES] = take_rows(values, order)

    for copy in to_far + own_x + passes + [core_copy] + y_copies + z_copies:
        copy.wait_send()


def per_device(intermediate, amplitudes, occ_irrep, vir_irrep):
    vmem = pltpu.VMEM
    f32 = jnp.float32
    return pl.pallas_call(
        kernel,
        out_shape=jax.ShapeDtypeStruct((16, 1024), f32),
        in_specs=[
            pl.BlockSpec(memory_space=pl.ANY),
            pl.BlockSpec(memory_space=pl.ANY),
            pl.BlockSpec(memory_space=vmem),
            pl.BlockSpec(memory_space=pltpu.SMEM),
        ],
        out_specs=pl.BlockSpec(memory_space=vmem),
        scratch_shapes=[
            vmem((1024, 1024), f32),
            vmem((128, 1024), f32),
            vmem((1024, LANES), f32),
            vmem((1024, LANES), f32),
            vmem((2, IRREPS, 64, LANES), f32),
            vmem((IRREPS, 64, LANES), f32),
            vmem((4, IRREPS, 16, LANES), f32),
            vmem((3, IRREPS, 16, LANES), f32),
            vmem((LANES, LANES), f32),
            vmem((7, 16, LANES), f32),
            pltpu.SemaphoreType.DMA((W_CHUNKS + 1,)),
            pltpu.SemaphoreType.DMA((3 + 4 * FAR_CHUNKS,)),
            pltpu.SemaphoreType.DMA((3 + 4 * FAR_CHUNKS,)),
            pltpu.SemaphoreType.DMA((11,)),
            pltpu.SemaphoreType.DMA((11,)),
            pltpu.SemaphoreType.REGULAR((2,)),
        ],
        compiler_params=pltpu.CompilerParams(
            collective_id=0, has_side_effects=True, vmem_limit_bytes=60 * 1024 * 1024
        ),
        name="cycle_contraction",
    )(intermediate, amplitudes, occ_irrep, vir_irrep)


def solution(mesh):
    return jax.shard_map(
        per_device,
        mesh=mesh,
        in_specs=(P("col", ("layer", "row")), P(("layer", "row", "col"), None), P(), P()),
        out_specs=P(("layer", "row"), "col"),
        check_vma=False,
    )
```

```python
import jax
import jax.numpy as jnp
from jax import lax
from jax.experimental import pallas as pl
from jax.experimental.pallas import tpu as pltpu
from jax.sharding import PartitionSpec as P

MESH = pl.DeviceIdType.MESH
OCC = 200
IRREPS = 8
LANES = 128
W_CHUNKS = 8
OPPOSITE_FIRST = (1, 0, 2)
FAR_CHUNKS = 2


def take_lanes(values, index):
    return jnp.take_along_axis(values, index, axis=1)


def take_rows(values, index):
    return jnp.take_along_axis(values, index, axis=0)


def run_tables(first, offset, occ_low, occ_high, vir_ref, sub):
    virtual = first // OCC
    orbital = first % OCC + offset
    wraps = orbital >= OCC
    orbital = jnp.where(wraps, orbital - OCC, orbital)
    low = take_lanes(occ_low, jnp.minimum(orbital, LANES - 1))
    high = take_lanes(occ_high, jnp.maximum(orbital - (OCC - LANES), 0))
    occupied = jnp.where(orbital < LANES, low, high)
    irrep = jnp.zeros_like(sub)
    place = jnp.zeros_like(sub)
    for s in range(IRREPS):
        here = vir_ref[IRREPS * virtual + s]
        after = vir_ref[IRREPS * (virtual + 1) + s]
        value = occupied ^ jnp.where(wraps, after, here)
        irrep = jnp.where(sub == s, value, irrep)
        place = jnp.where(value == sub, s, place)
    return irrep, place


def split(values):
    high = values.astype(jnp.bfloat16)
    low = (values - high.astype(jnp.float32)).astype(jnp.bfloat16)
    return high, low


def kernel(
    w_hbm, a_hbm, occ_hbm, vir_hbm, out_ref,
    occ_ref, vir_ref, w_raw, a_raw, a_all, w_c, part, core_in, y_out, y_in, z_out, z_in,
    load_sem, col_send, col_recv, red_send, red_recv, known,
):
    layer, row, col = lax.axis_index("layer"), lax.axis_index("row"), lax.axis_index("col")
    core, z_lo = row % 2, row // 2
    z_hi, x = col // 4, col % 4

    def at(layer_=layer, z_lo_=z_lo, core_=core, col_=col):
        return (layer_, z_lo_ * 2 + core_, col_)

    def signal(semaphore, peer):
        pl.semaphore_signal(semaphore, inc=1, device_id=peer, device_id_type=MESH)

    far_col = (1 - z_hi) * 4 + x
    far, middle = at(col_=far_col), at(z_lo_=z_lo + 4 - 8 * (z_lo // 4))
    x_peers = [at(col_=z_hi * 4 + (x + k) % 4) for k in range(1, 4)]
    y_peers = [at(layer_=(layer + k) % 4) for k in range(1, 4)]
    z_peers = [at(z_lo_=(z_lo + k) % 8) for k in range(1, 8)]
    core_peer = at(core_=1 - core)
    z_near = [at(z_lo_=z_lo + 1 - 2 * (z_lo % 2)), at(z_lo_=z_lo + 2 - 4 * (z_lo // 2 % 2)), middle]
    near = z_near + [core_peer, far] + x_peers + y_peers

    barrier = pltpu.get_barrier_semaphore()
    for peer in near:
        signal(barrier, peer)

    a_load = pltpu.make_async_copy(a_hbm, a_raw, load_sem.at[W_CHUNKS])
    occ_load = pltpu.make_async_copy(occ_hbm, occ_ref, load_sem.at[W_CHUNKS + 1])
    vir_load = pltpu.make_async_copy(vir_hbm, vir_ref, load_sem.at[W_CHUNKS + 2])
    for load in (vir_load, occ_load, a_load):
        load.start()
    chunk_rows = w_raw.shape[0] // W_CHUNKS

    def w_load(n):
        rows = pl.ds(pl.multiple_of(n * chunk_rows, chunk_rows), chunk_rows)
        return pltpu.make_async_copy(w_hbm.at[rows], w_raw.at[rows], load_sem.at[n])

    shape = (IRREPS, LANES)
    sub = lax.broadcasted_iota(jnp.int32, shape, 0)
    lane = lax.broadcasted_iota(jnp.int32, shape, 1)
    occ_load.wait()
    vir_load.wait()
    occ_low = jnp.broadcast_to(occ_ref[pl.ds(0, LANES)][None, :], shape)
    occ_high = jnp.broadcast_to(occ_ref[pl.ds(OCC - LANES, LANES)][None, :], shape)
    run_of = ((lane >> 4) & 3) * 32 + ((lane >> 1) & 7) * 4 + (lane >> 6) * 2 + (lane & 1)
    n_irrep, n_place = run_tables(0, run_of, occ_low, occ_high, vir_ref, sub)
    p_irrep, p_place = run_tables((layer * 16 + row) * LANES, lane, occ_low, occ_high, vir_ref, sub)

    def compact(raw_ref, first_row, irrep, place, run, lane_index, block):
        which = jnp.full(shape, run, jnp.int32)
        index = take_rows(lane_index, take_lanes(irrep, which))
        total = jnp.zeros(shape, jnp.float32)
        for k in range(IRREPS):
            values = raw_ref[pl.ds(first_row, IRREPS), pl.ds(k * LANES, LANES)]
            total = jnp.where(block == k, take_lanes(values, index), total)
        return take_rows(total, take_lanes(place, which))

    a_load.wait()
    for n in range(W_CHUNKS):
        w_load(n).start()
    n_index, n_block = 8 * (run_of & 15) + n_place, run_of >> 4

    def compact_a(j, _):
        rows = pl.multiple_of(j * IRREPS, IRREPS)
        a_all[pl.ds(pl.multiple_of(col * LANES + rows, IRREPS), IRREPS), :] = compact(
            a_raw, rows, p_irrep, p_place, 16 * col + j, n_index, n_block
        )
        return 0

    lax.fori_loop(0, 16, compact_a, 0, unroll=8)

    pl.semaphore_wait(barrier, len(near))

    far_rows = LANES // FAR_CHUNKS
    x_at, far_at, pass_at = 0, 3, 3 + FAR_CHUNKS

    def block(ref, c, n=None):
        start, rows = (0, LANES) if n is None else (n * far_rows, far_rows)
        return ref.at[pl.ds(pl.multiple_of(c * LANES + start, far_rows), rows)]

    def col_copy(source, target, n, peer):
        return pltpu.make_async_remote_copy(
            src_ref=source, dst_ref=target, send_sem=col_send.at[n], recv_sem=col_recv.at[n],
            device_id=peer, device_id_type=MESH,
        )

    to_far = [col_copy(block(a_all, col, n), block(a_all, col, n), far_at + n, far) for n in range(FAR_CHUNKS)]
    own_x = [col_copy(block(a_all, col), block(a_all, col), x_at + k, x_peers[k]) for k in range(3)]

    for copy in to_far:
        copy.start()
    for k in OPPOSITE_FIRST:
        own_x[k].start()
    for peer in z_near:
        signal(known.at[0], peer)

    m_irrep, m_place = run_tables(col * LANES, lane, occ_low, occ_high, vir_ref, sub)
    p_index, p_block = 8 * (lane & 15) + p_place, lane >> 4

    def compact_w(i, _):
        rows = pl.multiple_of(i * IRREPS, IRREPS)
        w_c[pl.ds(rows, IRREPS), :] = compact(w_raw, rows, m_irrep, m_place, i, p_index, p_block)
        return 0

    def compact_chunk(n, _):
        w_load(n).wait()
        runs = LANES // W_CHUNKS
        for i in range(runs):
            compact_w(n * runs + i, 0)
        return 0

    lax.fori_loop(0, W_CHUNKS, compact_chunk, 0)

    pl.semaphore_wait(known.at[0], len(z_near))
    for peer in z_near:
        signal(known.at[1], peer)

    passes = []
    for n in range(FAR_CHUNKS):
        col_copy(block(a_all, far_col, n), block(a_all, far_col, n), far_at + n, far).wait_recv()
        for k in OPPOSITE_FIRST:
            copy = col_copy(
                block(a_all, far_col, n), block(a_all, far_col, n), pass_at + 3 * n + k, x_peers[k]
            )
            copy.start()
            passes.append(copy)
    for k in range(3):
        source = (x + 3 - k) % 4
        mine = block(a_all, z_hi * 4 + source)
        col_copy(mine, mine, x_at + k, x_peers[k]).wait_recv()
        for n in range(FAR_CHUNKS):
            passed = block(a_all, (1 - z_hi) * 4 + source, n)
            col_copy(passed, passed, pass_at + 3 * n + k, x_peers[k]).wait_recv()

    def product(left, right):
        return lax.dot_general(left, right, (((1,), (1,)), ((), ())), preferred_element_type=jnp.float32)

    def multiply(left, g):
        high, low = split(left)
        w_high, w_low = split(w_c[pl.ds(g, LANES, stride=IRREPS), :])
        return product(low, w_high) + product(high, w_low) + product(high, w_high)

    def multiply_other(g, _):
        left = a_all[pl.ds(g, LANES, stride=IRREPS), :].T
        part[0, g] = multiply(jnp.where(core == 0, left[64:], left[:64]), g)
        part[1, g] = jnp.where(core == 0, left[:64], left[64:])
        return 0

    def multiply_own(g, _):
        part[1, g] = multiply(part[1, g], g)
        return 0

    half = IRREPS // 2

    def group(q):
        return pl.ds(q * half, half)

    def red_copy(source, target, n, peer):
        return pltpu.make_async_remote_copy(
            src_ref=source, dst_ref=target, send_sem=red_send.at[n], recv_sem=red_recv.at[n],
            device_id=peer, device_id_type=MESH,
        )

    core_copies = [red_copy(part.at[0, group(q)], core_in.at[group(q)], 11 * q, core_peer) for q in range(2)]
    for q in range(2):
        lax.fori_loop(q * half, (q + 1) * half, multiply_other, 0, unroll=2)
        core_copies[q].start()
    lax.fori_loop(0, IRREPS, multiply_own, 0, unroll=2)

    def add_core(g, _):
        total = part[1, g] + core_in[g]
        for k in range(4):
            y_out[k, g] = total[16 * k : 16 * k + 16]
        return 0

    y_copies = [
        [
            red_copy(y_out.at[(layer + k) % 4, group(q)], y_in.at[k - 1, group(q)], 11 * q + k, y_peers[k - 1])
            for k in range(1, 4)
        ]
        for q in range(2)
    ]
    for q in range(2):
        core_copies[q].wait_recv()
        lax.fori_loop(q * half, (q + 1) * half, add_core, 0)
        for k in OPPOSITE_FIRST:
            y_copies[q][k].start()

    pl.semaphore_wait(known.at[1], len(z_near))

    def z_rows(z):
        return pl.ds(pl.multiple_of(z * 8, 8), 8)

    z_copies = [
        [
            red_copy(z_out.at[q, z_rows((z_lo + k) % 8)], z_in.at[q, k - 1], 11 * q + 3 + k, z_peers[k - 1])
            for k in range(1, 8)
        ]
        for q in range(2)
    ]
    for q in range(2):
        for copy in y_copies[q]:
            copy.wait_recv()
        for n in range(half):
            g = q * half + n
            total = y_out[layer, g] + y_in[0, g] + y_in[1, g] + y_in[2, g]
            z_out[q, pl.ds(n, 16, stride=half), :] = total
        for copy in z_copies[q]:
            copy.start()

    totals = []
    for q in range(2):
        total = z_out[q, z_rows(z_lo), :]
        for k in range(7):
            z_copies[q][k].wait_recv()
            total = total + z_in[q, k]
        totals.append(total)

    first_lane = core * 64 + layer * 16 + z_lo * 2
    for e in range(2):
        mine = jnp.concatenate([total[half * e : half * e + half] for total in totals], axis=0)
        order = take_lanes(n_irrep, jnp.full(shape, first_lane + e, jnp.int32))
        for k in range(IRREPS):
            spread = 16 * k + (lane >> 3)
            kept = take_lanes(m_place, spread) == (lane & 7)
            values = jnp.where(kept, take_lanes(mine, spread), 0.0)
            out_ref[8 * e : 8 * e + 8, k * LANES : (k + 1) * LANES] = take_rows(values, order)

    for copy in to_far + own_x + passes + core_copies + y_copies[0] + y_copies[1] + z_copies[0] + z_copies[1]:
        copy.wait_send()


def per_device(intermediate, amplitudes, occ_irrep, vir_irrep):
    vmem = pltpu.VMEM
    f32 = jnp.float32
    return pl.pallas_call(
        kernel,
        out_shape=jax.ShapeDtypeStruct((16, 1024), f32),
        in_specs=[
            pl.BlockSpec(memory_space=pl.ANY),
            pl.BlockSpec(memory_space=pl.ANY),
            pl.BlockSpec(memory_space=pl.ANY),
            pl.BlockSpec(memory_space=pl.ANY),
        ],
        out_specs=pl.BlockSpec(memory_space=vmem),
        scratch_shapes=[
            vmem((200,), jnp.int32),
            pltpu.SMEM((1800,), jnp.int32),
            vmem((1024, 1024), f32),
            vmem((128, 1024), f32),
            vmem((1024, LANES), f32),
            vmem((1024, LANES), f32),
            vmem((2, IRREPS, 64, LANES), f32),
            vmem((IRREPS, 64, LANES), f32),
            vmem((4, IRREPS, 16, LANES), f32),
            vmem((3, IRREPS, 16, LANES), f32),
            vmem((2, 64, LANES), f32),
            vmem((2, 7, 8, LANES), f32),
            pltpu.SemaphoreType.DMA((W_CHUNKS + 3,)),
            pltpu.SemaphoreType.DMA((3 + 4 * FAR_CHUNKS,)),
            pltpu.SemaphoreType.DMA((3 + 4 * FAR_CHUNKS,)),
            pltpu.SemaphoreType.DMA((22,)),
            pltpu.SemaphoreType.DMA((22,)),
            pltpu.SemaphoreType.REGULAR((2,)),
        ],
        compiler_params=pltpu.CompilerParams(
            collective_id=0, has_side_effects=True, vmem_limit_bytes=60 * 1024 * 1024
        ),
        name="cycle_contraction",
    )(intermediate, amplitudes, occ_irrep, vir_irrep)


def solution(mesh):
    return jax.shard_map(
        per_device,
        mesh=mesh,
        in_specs=(P("col", ("layer", "row")), P(("layer", "row", "col"), None), P(), P()),
        out_specs=P(("layer", "row"), "col"),
        check_vma=False,
    )
```

```python
import jax
import jax.numpy as jnp
from jax import lax
from jax.experimental import pallas as pl
from jax.experimental.pallas import tpu as pltpu
from jax.sharding import PartitionSpec as P

MESH = pl.DeviceIdType.MESH
OCC = 200
IRREPS = 8
LANES = 128
W_CHUNKS = 8
OPPOSITE_FIRST = (1, 0, 2)
FAR_CHUNKS = 2


def take_lanes(values, index):
    return jnp.take_along_axis(values, index, axis=1)


def take_rows(values, index):
    return jnp.take_along_axis(values, index, axis=0)


def run_tables(first, offset, occ_low, occ_high, vir_ref, sub):
    virtual = first // OCC
    orbital = first % OCC + offset
    wraps = orbital >= OCC
    orbital = jnp.where(wraps, orbital - OCC, orbital)
    low = take_lanes(occ_low, jnp.minimum(orbital, LANES - 1))
    high = take_lanes(occ_high, jnp.maximum(orbital - (OCC - LANES), 0))
    occupied = jnp.where(orbital < LANES, low, high)
    irrep = jnp.zeros_like(sub)
    place = jnp.zeros_like(sub)
    for s in range(IRREPS):
        here = vir_ref[IRREPS * virtual + s]
        after = vir_ref[IRREPS * (virtual + 1) + s]
        value = occupied ^ jnp.where(wraps, after, here)
        irrep = jnp.where(sub == s, value, irrep)
        place = jnp.where(value == sub, s, place)
    return irrep, place


def split(values):
    high = values.astype(jnp.bfloat16)
    low = (values - high.astype(jnp.float32)).astype(jnp.bfloat16)
    return high, low


def kernel(
    w_hbm, a_hbm, occ_hbm, vir_hbm, sums_ref, order_ref, place_ref,
    occ_ref, vir_ref, w_raw, a_raw, a_all, w_c, part, core_in, y_out, y_in, z_out, z_in,
    load_sem, col_send, col_recv, red_send, red_recv, known,
):
    layer, row, col = lax.axis_index("layer"), lax.axis_index("row"), lax.axis_index("col")
    core, z_lo = row % 2, row // 2
    z_hi, x = col // 4, col % 4

    def at(layer_=layer, z_lo_=z_lo, core_=core, col_=col):
        return (layer_, z_lo_ * 2 + core_, col_)

    def signal(semaphore, peer):
        pl.semaphore_signal(semaphore, inc=1, device_id=peer, device_id_type=MESH)

    far_col = (1 - z_hi) * 4 + x
    far, middle = at(col_=far_col), at(z_lo_=z_lo + 4 - 8 * (z_lo // 4))
    x_peers = [at(col_=z_hi * 4 + (x + k) % 4) for k in range(1, 4)]
    y_peers = [at(layer_=(layer + k) % 4) for k in range(1, 4)]
    z_peers = [at(z_lo_=(z_lo + k) % 8) for k in range(1, 8)]
    core_peer = at(core_=1 - core)
    z_near = [at(z_lo_=z_lo + 1 - 2 * (z_lo % 2)), at(z_lo_=z_lo + 2 - 4 * (z_lo // 2 % 2)), middle]
    near = z_near + [core_peer, far] + x_peers + y_peers

    barrier = pltpu.get_barrier_semaphore()
    for peer in near:
        signal(barrier, peer)

    a_load = pltpu.make_async_copy(a_hbm, a_raw, load_sem.at[W_CHUNKS])
    occ_load = pltpu.make_async_copy(occ_hbm, occ_ref, load_sem.at[W_CHUNKS + 1])
    vir_load = pltpu.make_async_copy(vir_hbm, vir_ref, load_sem.at[W_CHUNKS + 2])
    for load in (vir_load, occ_load, a_load):
        load.start()
    chunk_rows = w_raw.shape[0] // W_CHUNKS

    def w_load(n):
        rows = pl.ds(pl.multiple_of(n * chunk_rows, chunk_rows), chunk_rows)
        return pltpu.make_async_copy(w_hbm.at[rows], w_raw.at[rows], load_sem.at[n])

    shape = (IRREPS, LANES)
    sub = lax.broadcasted_iota(jnp.int32, shape, 0)
    lane = lax.broadcasted_iota(jnp.int32, shape, 1)
    occ_load.wait()
    vir_load.wait()
    occ_low = jnp.broadcast_to(occ_ref[pl.ds(0, LANES)][None, :], shape)
    occ_high = jnp.broadcast_to(occ_ref[pl.ds(OCC - LANES, LANES)][None, :], shape)
    run_of = ((lane >> 4) & 3) * 32 + ((lane >> 1) & 7) * 4 + (lane >> 6) * 2 + (lane & 1)
    n_irrep, n_place = run_tables(0, run_of, occ_low, occ_high, vir_ref, sub)
    p_irrep, p_place = run_tables((layer * 16 + row) * LANES, lane, occ_low, occ_high, vir_ref, sub)

    def compact(raw_ref, first_row, irrep, place, run, lane_index, block):
        which = jnp.full(shape, run, jnp.int32)
        index = take_rows(lane_index, take_lanes(irrep, which))
        total = jnp.zeros(shape, jnp.float32)
        for k in range(IRREPS):
            values = raw_ref[pl.ds(first_row, IRREPS), pl.ds(k * LANES, LANES)]
            total = jnp.where(block == k, take_lanes(values, index), total)
        return take_rows(total, take_lanes(place, which))

    a_load.wait()
    for n in range(W_CHUNKS):
        w_load(n).start()
    n_index, n_block = 8 * (run_of & 15) + n_place, run_of >> 4

    def compact_a(j, _):
        rows = pl.multiple_of(j * IRREPS, IRREPS)
        a_all[pl.ds(pl.multiple_of(col * LANES + rows, IRREPS), IRREPS), :] = compact(
            a_raw, rows, p_irrep, p_place, 16 * col + j, n_index, n_block
        )
        return 0

    lax.fori_loop(0, 16, compact_a, 0, unroll=16)

    pl.semaphore_wait(barrier, len(near))

    far_rows = LANES // FAR_CHUNKS
    x_at, far_at, pass_at = 0, 3, 3 + FAR_CHUNKS

    def block(ref, c, n=None):
        start, rows = (0, LANES) if n is None else (n * far_rows, far_rows)
        return ref.at[pl.ds(pl.multiple_of(c * LANES + start, far_rows), rows)]

    def col_copy(source, target, n, peer):
        return pltpu.make_async_remote_copy(
            src_ref=source, dst_ref=target, send_sem=col_send.at[n], recv_sem=col_recv.at[n],
            device_id=peer, device_id_type=MESH,
        )

    to_far = [col_copy(block(a_all, col, n), block(a_all, col, n), far_at + n, far) for n in range(FAR_CHUNKS)]
    own_x = [col_copy(block(a_all, col), block(a_all, col), x_at + k, x_peers[k]) for k in range(3)]

    for copy in to_far:
        copy.start()
    for k in OPPOSITE_FIRST:
        own_x[k].start()
    for peer in z_near:
        signal(known.at[0], peer)

    m_irrep, m_place = run_tables(col * LANES, lane, occ_low, occ_high, vir_ref, sub)
    p_index, p_block = 8 * (lane & 15) + p_place, lane >> 4

    def compact_w(i, _):
        rows = pl.multiple_of(i * IRREPS, IRREPS)
        w_c[pl.ds(rows, IRREPS), :] = compact(w_raw, rows, m_irrep, m_place, i, p_index, p_block)
        return 0

    def compact_chunk(n, _):
        w_load(n).wait()
        runs = LANES // W_CHUNKS
        for i in range(runs):
            compact_w(n * runs + i, 0)
        return 0

    lax.fori_loop(0, W_CHUNKS, compact_chunk, 0)

    pl.semaphore_wait(known.at[0], len(z_near))
    for peer in z_near:
        signal(known.at[1], peer)

    passes = []
    for n in range(FAR_CHUNKS):
        col_copy(block(a_all, far_col, n), block(a_all, far_col, n), far_at + n, far).wait_recv()
        for k in OPPOSITE_FIRST:
            copy = col_copy(
                block(a_all, far_col, n), block(a_all, far_col, n), pass_at + 3 * n + k, x_peers[k]
            )
            copy.start()
            passes.append(copy)
    for k in range(3):
        source = (x + 3 - k) % 4
        mine = block(a_all, z_hi * 4 + source)
        col_copy(mine, mine, x_at + k, x_peers[k]).wait_recv()
        for n in range(FAR_CHUNKS):
            passed = block(a_all, (1 - z_hi) * 4 + source, n)
            col_copy(passed, passed, pass_at + 3 * n + k, x_peers[k]).wait_recv()

    def product(left, right):
        return lax.dot_general(left, right, (((1,), (1,)), ((), ())), preferred_element_type=jnp.float32)

    def multiply(left, g):
        high, low = split(left)
        w_high, w_low = split(w_c[pl.ds(g, LANES, stride=IRREPS), :])
        return product(low, w_high) + product(high, w_low) + product(high, w_high)

    def multiply_other(g, _):
        left = a_all[pl.ds(g, LANES, stride=IRREPS), :].T
        part[0, g] = multiply(jnp.where(core == 0, left[64:], left[:64]), g)
        part[1, g] = jnp.where(core == 0, left[:64], left[64:])
        return 0

    def multiply_own(g, _):
        part[1, g] = multiply(part[1, g], g)
        return 0

    half = IRREPS // 2

    def group(q):
        return pl.ds(q * half, half)

    def red_copy(source, target, n, peer):
        return pltpu.make_async_remote_copy(
            src_ref=source, dst_ref=target, send_sem=red_send.at[n], recv_sem=red_recv.at[n],
            device_id=peer, device_id_type=MESH,
        )

    core_copies = [red_copy(part.at[0, group(q)], core_in.at[group(q)], 11 * q, core_peer) for q in range(2)]
    for q in range(2):
        lax.fori_loop(q * half, (q + 1) * half, multiply_other, 0, unroll=2)
        core_copies[q].start()
    lax.fori_loop(0, IRREPS, multiply_own, 0, unroll=2)

    def add_core(g, _):
        total = part[1, g] + core_in[g]
        for k in range(4):
            y_out[k, g] = total[16 * k : 16 * k + 16]
        return 0

    y_copies = [
        [
            red_copy(y_out.at[(layer + k) % 4, group(q)], y_in.at[k - 1, group(q)], 11 * q + k, y_peers[k - 1])
            for k in range(1, 4)
        ]
        for q in range(2)
    ]
    for q in range(2):
        core_copies[q].wait_recv()
        lax.fori_loop(q * half, (q + 1) * half, add_core, 0)
        for k in OPPOSITE_FIRST:
            y_copies[q][k].start()

    pl.semaphore_wait(known.at[1], len(z_near))

    def z_rows(z):
        return pl.ds(pl.multiple_of(z * 8, 8), 8)

    z_copies = [
        [
            red_copy(z_out.at[q, z_rows((z_lo + k) % 8)], z_in.at[q, k - 1], 11 * q + 3 + k, z_peers[k - 1])
            for k in range(1, 8)
        ]
        for q in range(2)
    ]
    for q in range(2):
        for copy in y_copies[q]:
            copy.wait_recv()
        for n in range(half):
            g = q * half + n
            total = y_out[layer, g] + y_in[0, g] + y_in[1, g] + y_in[2, g]
            z_out[q, pl.ds(n, 16, stride=half), :] = total
        for copy in z_copies[q]:
            copy.start()

    first_lane = core * 64 + layer * 16 + z_lo * 2
    for e in range(2):
        order_ref[8 * e : 8 * e + 8, :] = take_lanes(n_irrep, jnp.full(shape, first_lane + e, jnp.int32))
    place_ref[...] = m_place
    totals = []
    for q in range(2):
        total = z_out[q, z_rows(z_lo), :]
        for k in range(7):
            z_copies[q][k].wait_recv()
            total = total + z_in[q, k]
        totals.append(total)

    for e in range(2):
        mine = [total[half * e : half * e + half] for total in totals]
        sums_ref[8 * e : 8 * e + 8, :] = jnp.concatenate(mine, axis=0)

    for copy in to_far + own_x + passes + core_copies + y_copies[0] + y_copies[1] + z_copies[0] + z_copies[1]:
        copy.wait_send()


def expand(sums_ref, order_ref, place_ref, out_ref):
    lane = lax.broadcasted_iota(jnp.int32, (IRREPS, LANES), 1)
    for k in range(IRREPS):
        spread = 16 * k + (lane >> 3)
        kept = take_lanes(place_ref[...], spread) == (lane & 7)
        for rows in (slice(0, 8), slice(8, 16)):
            values = jnp.where(kept, take_lanes(sums_ref[rows, :], spread), 0.0)
            out_ref[rows, k * LANES : (k + 1) * LANES] = take_rows(values, order_ref[rows, :])


def per_device(intermediate, amplitudes, occ_irrep, vir_irrep):
    vmem = pltpu.VMEM
    f32 = jnp.float32
    sums, order, place = pl.pallas_call(
        kernel,
        out_shape=[
            jax.ShapeDtypeStruct((16, LANES), f32),
            jax.ShapeDtypeStruct((16, LANES), jnp.int32),
            jax.ShapeDtypeStruct((IRREPS, LANES), jnp.int32),
        ],
        in_specs=[
            pl.BlockSpec(memory_space=pl.ANY),
            pl.BlockSpec(memory_space=pl.ANY),
            pl.BlockSpec(memory_space=pl.ANY),
            pl.BlockSpec(memory_space=pl.ANY),
        ],
        out_specs=[pl.BlockSpec(memory_space=vmem)] * 3,
        scratch_shapes=[
            vmem((200,), jnp.int32),
            pltpu.SMEM((1800,), jnp.int32),
            vmem((1024, 1024), f32),
            vmem((128, 1024), f32),
            vmem((1024, LANES), f32),
            vmem((1024, LANES), f32),
            vmem((2, IRREPS, 64, LANES), f32),
            vmem((IRREPS, 64, LANES), f32),
            vmem((4, IRREPS, 16, LANES), f32),
            vmem((3, IRREPS, 16, LANES), f32),
            vmem((2, 64, LANES), f32),
            vmem((2, 7, 8, LANES), f32),
            pltpu.SemaphoreType.DMA((W_CHUNKS + 3,)),
            pltpu.SemaphoreType.DMA((3 + 4 * FAR_CHUNKS,)),
            pltpu.SemaphoreType.DMA((3 + 4 * FAR_CHUNKS,)),
            pltpu.SemaphoreType.DMA((22,)),
            pltpu.SemaphoreType.DMA((22,)),
            pltpu.SemaphoreType.REGULAR((2,)),
        ],
        compiler_params=pltpu.CompilerParams(
            collective_id=0, has_side_effects=True, vmem_limit_bytes=60 * 1024 * 1024
        ),
        name="cycle_contraction",
    )(intermediate, amplitudes, occ_irrep, vir_irrep)
    return pl.pallas_call(
        expand,
        out_shape=jax.ShapeDtypeStruct((16, 1024), f32),
        in_specs=[pl.BlockSpec(memory_space=vmem)] * 3,
        out_specs=pl.BlockSpec(memory_space=vmem),
        name="expand_irreps",
    )(sums, order, place)


def solution(mesh):
    return jax.shard_map(
        per_device,
        mesh=mesh,
        in_specs=(P("col", ("layer", "row")), P(("layer", "row", "col"), None), P(), P()),
        out_specs=P(("layer", "row"), "col"),
        check_vma=False,
    )
```

```python
import jax
import jax.numpy as jnp
from jax import lax
from jax.experimental import pallas as pl
from jax.experimental.pallas import tpu as pltpu
from jax.sharding import PartitionSpec as P

MESH = pl.DeviceIdType.MESH
OCC = 200
IRREPS = 8
LANES = 128
W_CHUNKS = 8
OPPOSITE_FIRST = (1, 0, 2)
FAR_CHUNKS = 4


def take_lanes(values, index):
    return jnp.take_along_axis(values, index, axis=1)


def take_rows(values, index):
    return jnp.take_along_axis(values, index, axis=0)


def run_tables(first, offset, occ_low, occ_high, vir_ref, sub):
    virtual = first // OCC
    orbital = first % OCC + offset
    wraps = orbital >= OCC
    orbital = jnp.where(wraps, orbital - OCC, orbital)
    low = take_lanes(occ_low, jnp.minimum(orbital, LANES - 1))
    high = take_lanes(occ_high, jnp.maximum(orbital - (OCC - LANES), 0))
    occupied = jnp.where(orbital < LANES, low, high)
    irrep = jnp.zeros_like(sub)
    place = jnp.zeros_like(sub)
    for s in range(IRREPS):
        here = vir_ref[IRREPS * virtual + s]
        after = vir_ref[IRREPS * (virtual + 1) + s]
        value = occupied ^ jnp.where(wraps, after, here)
        irrep = jnp.where(sub == s, value, irrep)
        place = jnp.where(value == sub, s, place)
    return irrep, place


def split(values):
    high = values.astype(jnp.bfloat16)
    low = (values - high.astype(jnp.float32)).astype(jnp.bfloat16)
    return high, low


def kernel(
    w_hbm, a_hbm, occ_hbm, vir_hbm, sums_ref, order_ref, place_ref,
    occ_ref, vir_ref, w_raw, a_raw, a_all, w_c, part, core_in, y_out, y_in, z_out, z_in,
    load_sem, col_send, col_recv, red_send, red_recv, known,
):
    layer, row, col = lax.axis_index("layer"), lax.axis_index("row"), lax.axis_index("col")
    core, z_lo = row % 2, row // 2
    z_hi, x = col // 4, col % 4

    def at(layer_=layer, z_lo_=z_lo, core_=core, col_=col):
        return (layer_, z_lo_ * 2 + core_, col_)

    def signal(semaphore, peer):
        pl.semaphore_signal(semaphore, inc=1, device_id=peer, device_id_type=MESH)

    far_col = (1 - z_hi) * 4 + x
    far, middle = at(col_=far_col), at(z_lo_=z_lo + 4 - 8 * (z_lo // 4))
    x_peers = [at(col_=z_hi * 4 + (x + k) % 4) for k in range(1, 4)]
    y_peers = [at(layer_=(layer + k) % 4) for k in range(1, 4)]
    z_peers = [at(z_lo_=(z_lo + k) % 8) for k in range(1, 8)]
    core_peer = at(core_=1 - core)
    z_near = [at(z_lo_=z_lo + 1 - 2 * (z_lo % 2)), at(z_lo_=z_lo + 2 - 4 * (z_lo // 2 % 2)), middle]
    near = z_near + [core_peer, far] + x_peers + y_peers

    barrier = pltpu.get_barrier_semaphore()
    for peer in near:
        signal(barrier, peer)

    a_load = pltpu.make_async_copy(a_hbm, a_raw, load_sem.at[W_CHUNKS])
    occ_load = pltpu.make_async_copy(occ_hbm, occ_ref, load_sem.at[W_CHUNKS + 1])
    vir_load = pltpu.make_async_copy(vir_hbm, vir_ref, load_sem.at[W_CHUNKS + 2])
    for load in (vir_load, occ_load, a_load):
        load.start()
    chunk_rows = w_raw.shape[0] // W_CHUNKS

    def w_load(n):
        rows = pl.ds(pl.multiple_of(n * chunk_rows, chunk_rows), chunk_rows)
        return pltpu.make_async_copy(w_hbm.at[rows], w_raw.at[rows], load_sem.at[n])

    shape = (IRREPS, LANES)
    sub = lax.broadcasted_iota(jnp.int32, shape, 0)
    lane = lax.broadcasted_iota(jnp.int32, shape, 1)
    occ_load.wait()
    vir_load.wait()
    occ_low = jnp.broadcast_to(occ_ref[pl.ds(0, LANES)][None, :], shape)
    occ_high = jnp.broadcast_to(occ_ref[pl.ds(OCC - LANES, LANES)][None, :], shape)
    run_of = ((lane >> 4) & 3) * 32 + ((lane >> 1) & 7) * 4 + (lane >> 6) * 2 + (lane & 1)
    n_irrep, n_place = run_tables(0, run_of, occ_low, occ_high, vir_ref, sub)
    p_irrep, p_place = run_tables((layer * 16 + row) * LANES, lane, occ_low, occ_high, vir_ref, sub)

    def compact(raw_ref, first_row, irrep, place, run, lane_index, block):
        which = jnp.full(shape, run, jnp.int32)
        index = take_rows(lane_index, take_lanes(irrep, which))
        total = jnp.zeros(shape, jnp.float32)
        for k in range(IRREPS):
            values = raw_ref[pl.ds(first_row, IRREPS), pl.ds(k * LANES, LANES)]
            total = jnp.where(block == k, take_lanes(values, index), total)
        return take_rows(total, take_lanes(place, which))

    a_load.wait()
    for n in range(W_CHUNKS):
        w_load(n).start()
    n_index, n_block = 8 * (run_of & 15) + n_place, run_of >> 4

    def compact_a(j, _):
        rows = pl.multiple_of(j * IRREPS, IRREPS)
        a_all[pl.ds(pl.multiple_of(col * LANES + rows, IRREPS), IRREPS), :] = compact(
            a_raw, rows, p_irrep, p_place, 16 * col + j, n_index, n_block
        )
        return 0

    lax.fori_loop(0, 16, compact_a, 0, unroll=16)

    pl.semaphore_wait(barrier, len(near))

    far_rows = LANES // FAR_CHUNKS
    x_at, far_at, pass_at = 0, 3, 3 + FAR_CHUNKS

    def block(ref, c, n=None):
        start, rows = (0, LANES) if n is None else (n * far_rows, far_rows)
        return ref.at[pl.ds(pl.multiple_of(c * LANES + start, far_rows), rows)]

    def col_copy(source, target, n, peer):
        return pltpu.make_async_remote_copy(
            src_ref=source, dst_ref=target, send_sem=col_send.at[n], recv_sem=col_recv.at[n],
            device_id=peer, device_id_type=MESH,
        )

    to_far = [col_copy(block(a_all, col, n), block(a_all, col, n), far_at + n, far) for n in range(FAR_CHUNKS)]
    own_x = [col_copy(block(a_all, col), block(a_all, col), x_at + k, x_peers[k]) for k in range(3)]

    for copy in to_far:
        copy.start()
    for k in OPPOSITE_FIRST:
        own_x[k].start()
    for peer in z_near:
        signal(known.at[0], peer)

    m_irrep, m_place = run_tables(col * LANES, lane, occ_low, occ_high, vir_ref, sub)
    p_index, p_block = 8 * (lane & 15) + p_place, lane >> 4

    def compact_w(i, _):
        rows = pl.multiple_of(i * IRREPS, IRREPS)
        w_c[pl.ds(rows, IRREPS), :] = compact(w_raw, rows, m_irrep, m_place, i, p_index, p_block)
        return 0

    def compact_chunk(n, _):
        w_load(n).wait()
        runs = LANES // W_CHUNKS
        for i in range(runs):
            compact_w(n * runs + i, 0)
        return 0

    lax.fori_loop(0, W_CHUNKS, compact_chunk, 0)

    pl.semaphore_wait(known.at[0], len(z_near))
    for peer in z_near:
        signal(known.at[1], peer)

    passes = []
    for n in range(FAR_CHUNKS):
        col_copy(block(a_all, far_col, n), block(a_all, far_col, n), far_at + n, far).wait_recv()
        for k in OPPOSITE_FIRST:
            copy = col_copy(
                block(a_all, far_col, n), block(a_all, far_col, n), pass_at + 3 * n + k, x_peers[k]
            )
            copy.start()
            passes.append(copy)
    for k in range(3):
        source = (x + 3 - k) % 4
        mine = block(a_all, z_hi * 4 + source)
        col_copy(mine, mine, x_at + k, x_peers[k]).wait_recv()
        for n in range(FAR_CHUNKS):
            passed = block(a_all, (1 - z_hi) * 4 + source, n)
            col_copy(passed, passed, pass_at + 3 * n + k, x_peers[k]).wait_recv()

    def product(left, right):
        return lax.dot_general(left, right, (((1,), (1,)), ((), ())), preferred_element_type=jnp.float32)

    def multiply(left, g):
        high, low = split(left)
        w_high, w_low = split(w_c[pl.ds(g, LANES, stride=IRREPS), :])
        return product(low, w_high) + product(high, w_low) + product(high, w_high)

    def multiply_other(g, _):
        left = a_all[pl.ds(g, LANES, stride=IRREPS), :].T
        part[0, g] = multiply(jnp.where(core == 0, left[64:], left[:64]), g)
        part[1, g] = jnp.where(core == 0, left[:64], left[64:])
        return 0

    def multiply_own(g, _):
        part[1, g] = multiply(part[1, g], g)
        return 0

    half = IRREPS // 2

    def group(q):
        return pl.ds(q * half, half)

    def red_copy(source, target, n, peer):
        return pltpu.make_async_remote_copy(
            src_ref=source, dst_ref=target, send_sem=red_send.at[n], recv_sem=red_recv.at[n],
            device_id=peer, device_id_type=MESH,
        )

    core_copies = [red_copy(part.at[0, group(q)], core_in.at[group(q)], 11 * q, core_peer) for q in range(2)]
    for q in range(2):
        lax.fori_loop(q * half, (q + 1) * half, multiply_other, 0, unroll=2)
        core_copies[q].start()
    lax.fori_loop(0, IRREPS, multiply_own, 0, unroll=2)

    def add_core(g, _):
        total = part[1, g] + core_in[g]
        for k in range(4):
            y_out[k, g] = total[16 * k : 16 * k + 16]
        return 0

    y_copies = [
        [
            red_copy(y_out.at[(layer + k) % 4, group(q)], y_in.at[k - 1, group(q)], 11 * q + k, y_peers[k - 1])
            for k in range(1, 4)
        ]
        for q in range(2)
    ]
    for q in range(2):
        core_copies[q].wait_recv()
        lax.fori_loop(q * half, (q + 1) * half, add_core, 0)
        for k in OPPOSITE_FIRST:
            y_copies[q][k].start()

    pl.semaphore_wait(known.at[1], len(z_near))

    def z_rows(z):
        return pl.ds(pl.multiple_of(z * 8, 8), 8)

    z_copies = [
        [
            red_copy(z_out.at[q, z_rows((z_lo + k) % 8)], z_in.at[q, k - 1], 11 * q + 3 + k, z_peers[k - 1])
            for k in range(1, 8)
        ]
        for q in range(2)
    ]
    for q in range(2):
        for copy in y_copies[q]:
            copy.wait_recv()
        for n in range(half):
            g = q * half + n
            total = y_out[layer, g] + y_in[0, g] + y_in[1, g] + y_in[2, g]
            z_out[q, pl.ds(n, 16, stride=half), :] = total
        for copy in z_copies[q]:
            copy.start()

    first_lane = core * 64 + layer * 16 + z_lo * 2
    for e in range(2):
        order_ref[8 * e : 8 * e + 8, :] = take_lanes(n_irrep, jnp.full(shape, first_lane + e, jnp.int32))
    place_ref[...] = m_place
    totals = []
    for q in range(2):
        total = z_out[q, z_rows(z_lo), :]
        for k in range(7):
            z_copies[q][k].wait_recv()
            total = total + z_in[q, k]
        totals.append(total)

    for e in range(2):
        mine = [total[half * e : half * e + half] for total in totals]
        sums_ref[8 * e : 8 * e + 8, :] = jnp.concatenate(mine, axis=0)

    for copy in to_far + own_x + passes + core_copies + y_copies[0] + y_copies[1] + z_copies[0] + z_copies[1]:
        copy.wait_send()


def expand(sums_ref, order_ref, place_ref, out_ref):
    lane = lax.broadcasted_iota(jnp.int32, (IRREPS, LANES), 1)
    for k in range(IRREPS):
        spread = 16 * k + (lane >> 3)
        kept = take_lanes(place_ref[...], spread) == (lane & 7)
        for rows in (slice(0, 8), slice(8, 16)):
            values = jnp.where(kept, take_lanes(sums_ref[rows, :], spread), 0.0)
            out_ref[rows, k * LANES : (k + 1) * LANES] = take_rows(values, order_ref[rows, :])


def per_device(intermediate, amplitudes, occ_irrep, vir_irrep):
    vmem = pltpu.VMEM
    f32 = jnp.float32
    sums, order, place = pl.pallas_call(
        kernel,
        out_shape=[
            jax.ShapeDtypeStruct((16, LANES), f32),
            jax.ShapeDtypeStruct((16, LANES), jnp.int32),
            jax.ShapeDtypeStruct((IRREPS, LANES), jnp.int32),
        ],
        in_specs=[
            pl.BlockSpec(memory_space=pl.ANY),
            pl.BlockSpec(memory_space=pl.ANY),
            pl.BlockSpec(memory_space=pl.ANY),
            pl.BlockSpec(memory_space=pl.ANY),
        ],
        out_specs=[pl.BlockSpec(memory_space=vmem)] * 3,
        scratch_shapes=[
            vmem((200,), jnp.int32),
            pltpu.SMEM((1800,), jnp.int32),
            vmem((1024, 1024), f32),
            vmem((128, 1024), f32),
            vmem((1024, LANES), f32),
            vmem((1024, LANES), f32),
            vmem((2, IRREPS, 64, LANES), f32),
            vmem((IRREPS, 64, LANES), f32),
            vmem((4, IRREPS, 16, LANES), f32),
            vmem((3, IRREPS, 16, LANES), f32),
            vmem((2, 64, LANES), f32),
            vmem((2, 7, 8, LANES), f32),
            pltpu.SemaphoreType.DMA((W_CHUNKS + 3,)),
            pltpu.SemaphoreType.DMA((3 + 4 * FAR_CHUNKS,)),
            pltpu.SemaphoreType.DMA((3 + 4 * FAR_CHUNKS,)),
            pltpu.SemaphoreType.DMA((22,)),
            pltpu.SemaphoreType.DMA((22,)),
            pltpu.SemaphoreType.REGULAR((2,)),
        ],
        compiler_params=pltpu.CompilerParams(
            collective_id=0, has_side_effects=True, vmem_limit_bytes=60 * 1024 * 1024
        ),
        name="cycle_contraction",
    )(intermediate, amplitudes, occ_irrep, vir_irrep)
    return pl.pallas_call(
        expand,
        out_shape=jax.ShapeDtypeStruct((16, 1024), f32),
        in_specs=[pl.BlockSpec(memory_space=vmem)] * 3,
        out_specs=pl.BlockSpec(memory_space=vmem),
        name="expand_irreps",
    )(sums, order, place)


def solution(mesh):
    return jax.shard_map(
        per_device,
        mesh=mesh,
        in_specs=(P("col", ("layer", "row")), P(("layer", "row", "col"), None), P(), P()),
        out_specs=P(("layer", "row"), "col"),
        check_vma=False,
    )
```
